128 devices in a mesh: outer: 4 (over x), shard: 32 (over z, y, core).
Axes of the slice: x: 4, y: 4, z: 4, core: 2. Of those that a mesh axis runs over, the one named last changes fastest.
Arguments:
- acts: bfloat16 [16384, 4096], P(('outer', 'shard')), may hold values from -6 to 6
- grads: bfloat16 [16384, 14336], P(('outer', 'shard')), may hold values from -18 to 18
- basis: float32 [32, 4096], replicated, may hold values from -6 to 6
- error_in: bfloat16 [4, 4096, 14336], P('outer', None, 'shard'), may hold values from -3 to 3
- weight: float32 [4096, 14336], P('outer', 'shard'), may hold values from -0.3 to 0.3
- moment_one: float32 [4096, 14336], P('outer', 'shard'), may hold values from -0.3 to 0.3
- moment_two: float32 [4096, 14336], P('outer', 'shard'), may hold values from 0.0001 to 0.01
Outputs:
- basis_out: float32 [32, 4096], replicated
- error_out: bfloat16 [4, 4096, 14336], P('outer', None, 'shard')
- weight_out: float32 [4096, 14336], P('outer', 'shard')
- moment_one_out: float32 [4096, 14336], P('outer', 'shard')
- moment_two_out: float32 [4096, 14336], P('outer', 'shard')
The draws below stay inside these ranges and needn't reach their ends.
All inputs are finite; a program needn't handle non-finite values.
Results may differ from the reference program's by a relative error of at most 0.001.
Values may be sent and summed in bfloat16 or wider, within the bound.
No kernel may reach another device: no remote copies, remote signals or barrier semaphores. Data moves between devices by JAX's collectives and lax.ppermute only.
A program may use at most 192 MiB of HBM per device.

```python
import math
import jax
import jax.numpy as jnp
from jax import lax

D = 4096
FF = 14336
RANK = 32
TOK_DEV = 128
PODS = 4
TOKENS = 16384
N_OUTER = 4
N_SHARD = 32


def draw_grads(key, part):
    key = jax.random.fold_in(key, 7)
    scale_key, value_key = jax.random.split(key)
    scales = jnp.exp(jax.random.uniform(scale_key, (1, FF), jnp.float32, math.log(0.3), math.log(3.0)))
    values = jnp.clip(jax.random.normal(value_key, (TOKENS, FF), jnp.float32), -6.0, 6.0)
    return (values * scales).astype(jnp.bfloat16)


def levels(rng, shape, pieces, smallest, high):
    def one(dim, shards_of):
        heights = jax.random.uniform(jax.random.fold_in(jax.random.fold_in(rng, 6), dim), (shards_of,), jnp.float32, smallest / len(pieces), high / len(pieces))
        return jnp.repeat(jnp.exp(heights), shape[dim] // shards_of).reshape((-1,) + (1,) * (len(shape) - dim - 1))

    level = one(*pieces[0])
    for cut in pieces[1:]:
        level = level * one(*cut)
    return level


def noise(key, extent, width, bound, cuts=(), kind=jnp.bfloat16):
    entries = jax.random.normal(key, extent, jnp.float32) * width
    if len(cuts) > 0:
        entries = levels(key, extent, cuts, -0.22, 0.18) * entries
    return jnp.clip(entries, min=-bound, max=bound).astype(kind)


def setup_inputs(seed: int = 0) -> dict:
    key_list = jax.random.split(jax.random.key(seed), 8)
    acts = noise(key_list[0], (TOKENS, D), 1.0, 6.0, ((0, 128),))
    grads = draw_grads(jax.random.fold_in(key_list[7], 71), 0)
    basis = noise(key_list[2], (RANK, D), 1.0, 6.0, (), jnp.float32)
    error_in = noise(key_list[3], (PODS, D, FF), 0.5, 3.0, ((0, 4), (2, 32)))
    weight = noise(key_list[4], (D, FF), 0.05, 0.3, ((0, 4), (1, 32)), jnp.float32)
    moment_one = noise(key_list[5], (D, FF), 0.05, 0.3, ((0, 4), (1, 32)), jnp.float32)
    moment_two = jnp.clip(jnp.exp(math.log(0.01) - 4.6051702 * jax.random.uniform(key_list[6], (D, FF), jnp.float32) ** levels(key_list[6], (D, FF), ((0, 4), (1, 32)), -0.2, 0.2)), 0.0001, 0.01)
    return dict(acts=acts, grads=grads, basis=basis, error_in=error_in, weight=weight, moment_one=moment_one, moment_two=moment_two)


beta_one = 0.9
beta_two = 0.95
learn_rate = 0.01
decay_rate = 0.1
adam_epsilon = 1e-08
first_fix = 1.0 - 0.9 ** 8
second_fix = 1.0 - 0.95 ** 8

def reference(acts, grads, basis, error_in, weight, moment_one, moment_two):
    tok_pod = TOK_DEV * N_SHARD
    factor_scale = tok_pod ** (-0.5)
    highest = lax.Precision.HIGHEST
    matrices = []
    factor = jnp.zeros((RANK, FF), jnp.float32)
    for pod in range(N_OUTER):
        pod_acts = acts[pod * tok_pod:(pod + 1) * tok_pod]
        pod_grads = grads[pod * tok_pod:(pod + 1) * tok_pod]
        gradient = lax.dot_general(pod_acts.astype(jnp.float32), pod_grads.astype(jnp.float32), (((0,), (0,)), ((), ())), preferred_element_type=jnp.float32) * factor_scale
        matrix = gradient + error_in[pod].astype(jnp.float32)
        matrices.append(matrix)
        factor = factor + jnp.dot(basis, matrix, precision=highest)
    factor = factor / N_OUTER
    gram = jnp.dot(factor, factor.T, precision=highest)
    lower = jnp.linalg.cholesky(gram)
    ortho = jax.scipy.linalg.solve_triangular(lower, factor, lower=True)
    basis_out = jnp.zeros((RANK, D), jnp.float32)
    for pod in range(N_OUTER):
        basis_out = basis_out + lax.dot_general(ortho, matrices[pod], (((1,), (1,)), ((), ())), precision=highest)
    basis_out = basis_out / N_OUTER
    approx = lax.dot_general(basis_out, ortho, (((0,), (0,)), ((), ())), precision=highest)
    error_out = jnp.stack([(matrix - approx).astype(jnp.bfloat16) for matrix in matrices])
    moment_one_out = beta_one * moment_one + (1.0 - beta_one) * approx
    moment_two_out = beta_two * moment_two + (1.0 - beta_two) * approx * approx
    step_size = moment_one_out / first_fix / (jnp.sqrt(moment_two_out / second_fix) + adam_epsilon)
    weight_out = weight * (1.0 - learn_rate * decay_rate) - learn_rate * step_size
    return (basis_out, error_out, weight_out, moment_one_out, moment_two_out)
```

```python
import jax
import jax.numpy as jnp
from jax import lax
from jax.sharding import Mesh, PartitionSpec as P

beta_one = 0.9
beta_two = 0.95
learn_rate = 0.01
decay_rate = 0.1
adam_epsilon = 1e-08
first_fix = 1.0 - 0.9**8
second_fix = 1.0 - 0.95**8

SHARD = ("z", "y", "core")
ALL = ("outer", "z", "y", "core")


def split3(x):
    high = lax.reduce_precision(x, 8, 7)
    rest = x - high
    middle = lax.reduce_precision(rest, 8, 7)
    return [p.astype(jnp.bfloat16) for p in (high, middle, rest - middle)]


def swap(x, axis, k):
    n = lax.axis_size(axis)
    return lax.ppermute(x, axis, [(i, i ^ k) for i in range(n)])


def sum4(x, axis):
    a, b, c = swap(x, axis, 1), swap(x, axis, 2), swap(x, axis, 3)
    return (x + a) + (b + c)


def dot(a, b, ca, cb):
    return lax.dot_general(a, b, (((ca,), (cb,)), ((), ())), preferred_element_type=jnp.float32)


def thrice(x, b, cb):
    r = x.shape[0]
    y = dot(jnp.concatenate(split3(x), 0), b, 1, cb)
    return y[:r] + y[r : 2 * r] + y[2 * r :]


def per_device(acts, grads, basis, error_in, weight, moment_one, moment_two):
    highest = lax.Precision.HIGHEST
    shards = lax.axis_size(SHARD)
    devices = lax.axis_size(ALL)
    pods = lax.axis_size("outer")
    tok, width = acts.shape
    cols = error_in.shape[2]
    rank = basis.shape[0]
    scale = (tok * shards) ** (-0.5)
    half = width // 2
    gathered = [lax.all_gather(acts[:, i * half : (i + 1) * half], SHARD, axis=0, tiled=True) for i in range(2)]

    error_t = error_in[0].T
    proj = thrice(basis, acts, 1) * scale
    proj_all = lax.all_to_all(jnp.broadcast_to(proj[None], (shards, rank, tok)), SHARD, 0, 0)
    base = thrice(basis, error_t, 1)
    got = lax.all_to_all(grads.T.reshape(shards, cols, tok), SHARD, 0, 0)
    got_t = got.transpose(1, 0, 2).reshape(cols, shards * tok)

    proj_all = proj_all.transpose(1, 0, 2).reshape(rank, shards * tok)
    factor = sum4(thrice(proj_all, got_t, 1) + base, "outer") / pods
    gram = jnp.dot(factor, factor.T, precision=highest)
    gram = gram + swap(gram, "core", 1)
    gram = sum4(gram, "y")
    gram = sum4(gram, "z")
    lower = jnp.linalg.cholesky(gram)
    ortho = jax.scipy.linalg.solve_triangular(lower, factor, lower=True)

    wide = thrice(ortho, got_t, 0)
    wide = lax.all_to_all(wide.reshape(rank, shards, tok).transpose(1, 0, 2), SHARD, 0, 0)
    inner = wide.sum(0) * scale
    terms = thrice(inner, acts, 0) + thrice(ortho, error_t, 0)
    piece = lax.all_to_all(terms.reshape(devices, -1), ALL, 0, 0, tiled=True).sum(0) / pods
    basis_out = lax.all_to_all(jnp.broadcast_to(piece[None], (devices, piece.shape[0])), ALL, 0, 0, tiled=True)
    basis_out = basis_out.reshape(rank, width)

    approx_t = lax.dot_general(ortho, basis_out, (((0,), (0,)), ((), ())), precision=highest)
    outs = []
    for i in range(2):
        part = slice(i * half, (i + 1) * half)
        gradient = dot(got_t, gathered[i], 1, 0) * scale
        outs.append((gradient + error_t[:, part].astype(jnp.float32) - approx_t[:, part]).astype(jnp.bfloat16))
    error_out = jnp.concatenate(outs, 1).T[None]

    own_rows = weight.shape[0]
    row_start = lax.axis_index("outer") * own_rows
    update = lax.dynamic_slice_in_dim(approx_t, row_start, own_rows, 1).T
    moment_one_out = beta_one * moment_one + (1.0 - beta_one) * update
    moment_two_out = beta_two * moment_two + (1.0 - beta_two) * update * update
    step_size = moment_one_out / first_fix / (jnp.sqrt(moment_two_out / second_fix) + adam_epsilon)
    weight_out = weight * (1.0 - learn_rate * decay_rate) - learn_rate * step_size
    return (basis_out, error_out, weight_out, moment_one_out, moment_two_out)


def solution(mesh):
    devices = mesh.devices
    mesh = Mesh(devices.reshape(devices.shape[0], 4, 4, -1), ALL)
    tokens = P(ALL, None)
    state = P("outer", SHARD)
    errors = P("outer", None, SHARD)
    return jax.shard_map(
        per_device,
        mesh=mesh,
        in_specs=(tokens, tokens, P(), errors, state, state, state),
        out_specs=(P(), errors, state, state, state),
        check_vma=False,
    )
```

```python
import jax
import jax.numpy as jnp
from jax import lax
from jax.experimental import pallas as pl
from jax.experimental.pallas import tpu as pltpu
from jax.sharding import Mesh, PartitionSpec as P

beta_one = 0.9
beta_two = 0.95
learn_rate = 0.01
decay_rate = 0.1
adam_epsilon = 1e-08
first_fix = 1.0 - 0.9**8
second_fix = 1.0 - 0.95**8

SHARD = ("z", "y", "core")
ALL = ("outer", "z", "y", "core")
CHIPS = ("outer", "z", "y")
VMEM_LIMIT = 48 * 1024 * 1024


def split3(x):
    high = lax.reduce_precision(x, 8, 7)
    rest = x - high
    middle = lax.reduce_precision(rest, 8, 7)
    return [p.astype(jnp.bfloat16) for p in (high, middle, rest - middle)]


def dot(a, b, ca, cb):
    return lax.dot_general(a, b, (((ca,), (cb,)), ((), ())), preferred_element_type=jnp.float32)


def thrice(x, b, cb):
    r = x.shape[0]
    y = dot(jnp.concatenate(split3(x), 0), b, 1, cb)
    return y[:r] + y[r : 2 * r] + y[2 * r :]


def swap(x, axis, k):
    return lax.ppermute(x, axis, [(i, i ^ k) for i in range(lax.axis_size(axis))])


def twin(x):
    return swap(x, "core", 1)


def sum4(x, axis):
    a, b, c = swap(x, axis, 1), swap(x, axis, 2), swap(x, axis, 3)
    return (x + a) + (b + c)


def pick(x, i, axis):
    return lax.dynamic_index_in_dim(x, i, axis, keepdims=False)


def scatter4(x, axis, dim):
    i = lax.axis_index(axis)
    a, b, c = (swap(pick(x, i ^ k, dim), axis, k) for k in (1, 2, 3))
    return (pick(x, i, dim) + a) + (b + c)


def gather_axis(x, axis):
    n = lax.axis_size(axis)
    i = lax.axis_index(axis)
    x = jnp.stack([x] + [swap(x, axis, k) for k in range(1, n)])
    bit = 1
    while bit < n:
        y = x.reshape((n // (2 * bit), 2, bit) + x.shape[1:])
        x = jnp.where((i & bit) != 0, y[:, ::-1], y).reshape(x.shape)
        bit *= 2
    return x


def project(core, factor3, got):
    shards, cols, tok = got.shape
    rank = factor3.shape[0] // 3
    chips = shards // 2
    step = min(4, chips)

    def body(c, f_ref, g_ref, keep_ref, send_ref):
        own = c[0] == 0
        for k in range(step):
            pair = jnp.concatenate([g_ref[2 * k], g_ref[2 * k + 1]], axis=1)
            y = jnp.dot(f_ref[...], pair, preferred_element_type=jnp.float32)
            y = y[:rank] + y[rank : 2 * rank] + y[2 * rank :]
            first, second = y[:, :tok], y[:, tok:]
            keep_ref[k] = jnp.where(own, first, second)
            send_ref[k] = jnp.where(own, second, first)

    block = pl.BlockSpec((step, rank, tok), lambda n, c: (n, 0, 0))
    return pl.pallas_call(
        body,
        out_shape=[jax.ShapeDtypeStruct((chips, rank, tok), jnp.float32)] * 2,
        grid_spec=pltpu.PrefetchScalarGridSpec(
            num_scalar_prefetch=1,
            grid=(chips // step,),
            in_specs=[
                pl.BlockSpec((3 * rank, cols), lambda n, c: (0, 0)),
                pl.BlockSpec((2 * step, cols, tok), lambda n, c: (n, 0, 0)),
            ],
            out_specs=[block, block],
        ),
        compiler_params=pltpu.CompilerParams(vmem_limit_bytes=VMEM_LIMIT),
        cost_estimate=pl.CostEstimate(flops=6 * rank * cols * shards * tok, bytes_accessed=2 * shards * cols * tok, transcendentals=0),
    )(core, factor3, got)


def finish(place, ortho6, basis6, matrix, weight, moment_one, moment_two):
    cols, rows = weight.shape
    width = matrix.shape[1]
    steps = min(8, width // 128)
    block = width // steps
    small = rows // steps
    depth6 = ortho6.shape[1]

    def body(p, ortho_ref, basis_ref, own_ref, matrix_ref, w_ref, one_ref, two_ref, e_out, w_out, one_out, two_out):
        approx = jnp.dot(ortho_ref[...], basis_ref[...], preferred_element_type=jnp.float32)
        e_out[...] = (matrix_ref[...] - approx).astype(jnp.bfloat16)
        update = jnp.dot(ortho_ref[...], own_ref[...], preferred_element_type=jnp.float32)
        one = beta_one * one_ref[...] + (1.0 - beta_one) * update
        two = beta_two * two_ref[...] + (1.0 - beta_two) * update * update
        step = one / first_fix / (jnp.sqrt(two / second_fix) + adam_epsilon)
        w_out[...] = w_ref[...] * (1.0 - learn_rate * decay_rate) - learn_rate * step
        one_out[...] = one
        two_out[...] = two

    own = pl.BlockSpec((cols, small), lambda n, p: (0, n))
    wide = pl.BlockSpec((cols, block), lambda n, p: (0, n))
    return pl.pallas_call(
        body,
        out_shape=[jax.ShapeDtypeStruct(matrix.shape, jnp.bfloat16)] + [jax.ShapeDtypeStruct(weight.shape, jnp.float32)] * 3,
        grid_spec=pltpu.PrefetchScalarGridSpec(
            num_scalar_prefetch=1,
            grid=(steps,),
            in_specs=[
                pl.BlockSpec((cols, depth6), lambda n, p: (0, 0)),
                pl.BlockSpec((depth6, block), lambda n, p: (0, n)),
                pl.BlockSpec((depth6, small), lambda n, p: (0, p[0] * steps + n)),
                wide,
                own,
                own,
                own,
            ],
            out_specs=[wide, own, own, own],
        ),
        compiler_params=pltpu.CompilerParams(vmem_limit_bytes=VMEM_LIMIT),
        cost_estimate=pl.CostEstimate(
            flops=2 * cols * (rows + width) * depth6, bytes_accessed=24 * cols * rows + 6 * cols * width, transcendentals=cols * rows
        ),
    )(place, ortho6, basis6, basis6, matrix, weight, moment_one, moment_two)


def per_device(acts, grads, basis, error_in, weight, moment_one, moment_two):
    highest = lax.Precision.HIGHEST
    shards = lax.axis_size(SHARD)
    chips = lax.axis_size(CHIPS)
    pods = lax.axis_size("outer")
    tok, width = acts.shape
    cols = error_in.shape[2]
    rank = basis.shape[0]
    scale = (tok * shards) ** (-0.5)
    core = lax.axis_index("core")
    error_t = error_in[0].T
    gathered = lax.all_gather(acts, SHARD, axis=0, tiled=True)

    proj = gather_axis(gather_axis(thrice(basis, acts, 1) * scale, "core"), "y")
    grads_t, proj = lax.optimization_barrier((grads.T.reshape(shards, cols, tok), proj))
    got = lax.all_to_all(grads_t, SHARD, 0, 0)
    got_t = got.transpose(1, 0, 2).reshape(cols, shards * tok)
    proj = gather_axis(proj, "z").reshape(shards, rank, tok).transpose(1, 0, 2).reshape(rank, shards * tok)
    base = thrice(basis, error_t, 1)

    factor = sum4(thrice(proj, got_t, 1) + base, "outer") / pods
    factor3 = jnp.concatenate(split3(factor), 0)
    keep, send = project(core.astype(jnp.int32).reshape(1), factor3, got)
    inner = (keep + twin(send)).reshape(4, 4, rank, tok)
    inner = scatter4(scatter4(inner, "y", 1), "z", 0) * scale
    terms = thrice(inner, acts, 0) + thrice(factor, error_t, 0)
    rows = rank // 2
    mine = lax.dynamic_slice_in_dim(terms, core * rows, rows, 0)
    other = lax.dynamic_slice_in_dim(terms, (1 - core) * rows, rows, 0)
    tiles = (rows // 8, 8, width // 128, 128)
    mine = (mine + twin(other)).reshape(tiles).transpose(0, 2, 1, 3).reshape(chips, -1, 128)
    piece = lax.all_to_all(mine, CHIPS, 0, 0, tiled=True).sum(0) / pods
    mine = lax.all_to_all(jnp.broadcast_to(piece[None], mine.shape), CHIPS, 0, 0, tiled=True)
    other = twin(mine)
    terms = jnp.concatenate([jnp.where(core == 0, mine, other), jnp.where(core == 0, other, mine)], 0)
    terms = terms.reshape(rank // 8, width // 128, 8, 128).transpose(0, 2, 1, 3).reshape(rank, width)

    gram = jnp.dot(factor, factor.T, precision=highest)
    gram = gram + twin(gram)
    gram = sum4(sum4(gram, "y"), "z")
    lower = jnp.linalg.cholesky(gram)
    inverse = jax.scipy.linalg.solve_triangular(lower, jnp.eye(rank, dtype=jnp.float32), lower=True)
    ortho = jnp.dot(inverse, factor, precision=highest)
    basis_out = jnp.dot(inverse, terms, precision=highest)

    oh, om, ol = split3(ortho)
    bh, bm, bl = split3(basis_out)
    ortho6 = jnp.concatenate([oh, oh, om, oh, ol, om], 0).T
    basis6 = jnp.concatenate([bh, bm, bh, bl, bh, bm], 0)

    matrix = dot(got_t, gathered, 1, 0) * scale + error_t.astype(jnp.float32)
    place = lax.axis_index("outer").astype(jnp.int32).reshape(1)
    error_out, *state = finish(place, ortho6, basis6, matrix, weight.T, moment_one.T, moment_two.T)
    return (basis_out, error_out.T[None], state[0].T, state[1].T, state[2].T)


def solution(mesh):
    devices = mesh.devices
    mesh = Mesh(devices.reshape(devices.shape[0], 4, 4, -1), ALL)
    tokens = P(ALL, None)
    state = P("outer", SHARD)
    errors = P("outer", None, SHARD)
    return jax.shard_map(
        per_device,
        mesh=mesh,
        in_specs=(tokens, tokens, P(), errors, state, state, state),
        out_specs=(P(), errors, state, state, state),
        check_vma=False,
    )
```

```python
import jax
import jax.numpy as jnp
from jax import lax
from jax.experimental import pallas as pl
from jax.experimental.pallas import tpu as pltpu
from jax.sharding import Mesh, PartitionSpec as P

beta_one = 0.9
beta_two = 0.95
learn_rate = 0.01
decay_rate = 0.1
adam_epsilon = 1e-08
first_fix = 1.0 - 0.9**8
second_fix = 1.0 - 0.95**8

SHARD = ("z", "y", "core")
ALL = ("outer", "z", "y", "core")
CHIPS = ("outer", "z", "y")
VMEM_LIMIT = 48 * 1024 * 1024


def split3(x):
    high = lax.reduce_precision(x, 8, 7)
    rest = x - high
    middle = lax.reduce_precision(rest, 8, 7)
    return [p.astype(jnp.bfloat16) for p in (high, middle, rest - middle)]


def dot(a, b, ca, cb):
    return lax.dot_general(a, b, (((ca,), (cb,)), ((), ())), preferred_element_type=jnp.float32)


def thrice(x, b, cb):
    r = x.shape[0]
    y = dot(jnp.concatenate(split3(x), 0), b, 1, cb)
    return y[:r] + y[r : 2 * r] + y[2 * r :]


def swap(x, axis, k):
    return lax.ppermute(x, axis, [(i, i ^ k) for i in range(lax.axis_size(axis))])


def twin(x):
    return swap(x, "core", 1)


def sum4(x, axis):
    a, b, c = swap(x, axis, 1), swap(x, axis, 2), swap(x, axis, 3)
    return (x + a) + (b + c)


def gather_axis(x, axis):
    n = lax.axis_size(axis)
    i = lax.axis_index(axis)
    x = jnp.stack([x] + [swap(x, axis, k) for k in range(1, n)])
    bit = 1
    while bit < n:
        y = x.reshape((n // (2 * bit), 2, bit) + x.shape[1:])
        x = jnp.where((i & bit) != 0, y[:, ::-1], y).reshape(x.shape)
        bit *= 2
    return x


def parts3(x):
    high = x.astype(jnp.bfloat16)
    rest = x - high.astype(jnp.float32)
    middle = rest.astype(jnp.bfloat16)
    return high, middle, (rest - middle.astype(jnp.float32)).astype(jnp.bfloat16)


def project(core, factor, factor3, got):
    shards, cols, tok = got.shape
    rank = factor.shape[0]
    chips = shards // 2
    step = min(4, chips)

    def body(c, f_ref, f3_ref, g_ref, keep_ref, send_ref, gram_ref):
        own = c[0] == 0

        @pl.when(pl.program_id(0) == 0)
        def _():
            h, m, l = parts3(f_ref[...])
            gram = dot(h, l, 1, 1) + dot(l, h, 1, 1) + dot(m, m, 1, 1)
            gram = gram + (dot(h, m, 1, 1) + dot(m, h, 1, 1)) + dot(h, h, 1, 1)
            gram_ref[...] = jnp.concatenate([gram, jnp.zeros((rank, tok - rank), jnp.float32)], axis=1)

        for k in range(step):
            pair = jnp.concatenate([g_ref[2 * k], g_ref[2 * k + 1]], axis=1)
            y = jnp.dot(f3_ref[...], pair, preferred_element_type=jnp.float32)
            y = y[:rank] + y[rank : 2 * rank] + y[2 * rank :]
            first, second = y[:, :tok], y[:, tok:]
            keep_ref[k, :rank] = jnp.where(own, first, second)
            send_ref[k, :rank] = jnp.where(own, second, first)
            keep_ref[k, rank:] = gram_ref[...]
            send_ref[k, rank:] = gram_ref[...]

    block = pl.BlockSpec((step, 2 * rank, tok), lambda n, c: (n, 0, 0))
    return pl.pallas_call(
        body,
        out_shape=[jax.ShapeDtypeStruct((chips, 2 * rank, tok), jnp.float32)] * 2,
        grid_spec=pltpu.PrefetchScalarGridSpec(
            num_scalar_prefetch=1,
            grid=(chips // step,),
            in_specs=[
                pl.BlockSpec((rank, cols), lambda n, c: (0, 0)),
                pl.BlockSpec((3 * rank, cols), lambda n, c: (0, 0)),
                pl.BlockSpec((2 * step, cols, tok), lambda n, c: (n, 0, 0)),
            ],
            out_specs=[block, block],
            scratch_shapes=[pltpu.VMEM((rank, tok), jnp.float32)],
        ),
        compiler_params=pltpu.CompilerParams(vmem_limit_bytes=VMEM_LIMIT),
        cost_estimate=pl.CostEstimate(flops=6 * rank * cols * shards * tok, bytes_accessed=2 * shards * cols * tok, transcendentals=0),
    )(core, factor, factor3, got)


def finish_error(got, gathered, error_t, ortho6, basis6, scale):
    shards, cols, tok = got.shape
    tokens, width = gathered.shape
    block = min(1024, width)
    depth6 = ortho6.shape[1]

    def body(got_ref, acts_ref, error_ref, ortho_ref, basis_ref, out_ref, columns):
        @pl.when(pl.program_id(0) == 0)
        def _():
            for s in range(shards):
                columns[:, s * tok : (s + 1) * tok] = got_ref[s]

        gradient = jnp.dot(columns[...], acts_ref[...], preferred_element_type=jnp.float32)
        approx = jnp.dot(ortho_ref[...], basis_ref[...], preferred_element_type=jnp.float32)
        matrix = gradient * scale + error_ref[...].astype(jnp.float32)
        out_ref[...] = (matrix - approx).astype(jnp.bfloat16)

    wide = pl.BlockSpec((cols, block), lambda n: (0, n))
    return pl.pallas_call(
        body,
        out_shape=jax.ShapeDtypeStruct(error_t.shape, jnp.bfloat16),
        grid=(width // block,),
        in_specs=[
            pl.BlockSpec((shards, cols, tok), lambda n: (0, 0, 0)),
            pl.BlockSpec((tokens, block), lambda n: (0, n)),
            wide,
            pl.BlockSpec((cols, depth6), lambda n: (0, 0)),
            pl.BlockSpec((depth6, block), lambda n: (0, n)),
        ],
        out_specs=wide,
        scratch_shapes=[pltpu.VMEM((cols, tokens), got.dtype)],
        compiler_params=pltpu.CompilerParams(vmem_limit_bytes=VMEM_LIMIT),
        cost_estimate=pl.CostEstimate(
            flops=2 * cols * width * (tokens + depth6), bytes_accessed=2 * tokens * (width + cols) + 4 * cols * width, transcendentals=0
        ),
    )(got, gathered, error_t, ortho6, basis6)


def adam(place, ortho6, basis6, weight, moment_one, moment_two):
    cols, rows = weight.shape
    block = min(256, rows)
    steps = rows // block
    depth6 = ortho6.shape[1]

    def body(p, ortho_ref, basis_ref, w_ref, one_ref, two_ref, w_out, one_out, two_out):
        update = jnp.dot(ortho_ref[...], basis_ref[...], preferred_element_type=jnp.float32)
        one = beta_one * one_ref[...] + (1.0 - beta_one) * update
        two = beta_two * two_ref[...] + (1.0 - beta_two) * update * update
        step = one / first_fix / (jnp.sqrt(two / second_fix) + adam_epsilon)
        w_out[...] = w_ref[...] * (1.0 - learn_rate * decay_rate) - learn_rate * step
        one_out[...] = one
        two_out[...] = two

    own = pl.BlockSpec((cols, block), lambda n, p: (0, n))
    return pl.pallas_call(
        body,
        out_shape=[jax.ShapeDtypeStruct(weight.shape, jnp.float32)] * 3,
        grid_spec=pltpu.PrefetchScalarGridSpec(
            num_scalar_prefetch=1,
            grid=(steps,),
            in_specs=[
                pl.BlockSpec((cols, depth6), lambda n, p: (0, 0)),
                pl.BlockSpec((depth6, block), lambda n, p: (0, p[0] * steps + n)),
                own,
                own,
                own,
            ],
            out_specs=[own, own, own],
        ),
        compiler_params=pltpu.CompilerParams(vmem_limit_bytes=VMEM_LIMIT),
        cost_estimate=pl.CostEstimate(flops=2 * cols * rows * depth6, bytes_accessed=24 * cols * rows, transcendentals=cols * rows),
    )(place, ortho6, basis6, weight, moment_one, moment_two)


def per_device(acts, grads, basis, error_in, weight, moment_one, moment_two):
    highest = lax.Precision.HIGHEST
    shards = lax.axis_size(SHARD)
    chips = lax.axis_size(CHIPS)
    pods = lax.axis_size("outer")
    tok, width = acts.shape
    cols = error_in.shape[2]
    rank = basis.shape[0]
    scale = (tok * shards) ** (-0.5)
    core = lax.axis_index("core")
    error_t = error_in[0].T
    gathered = lax.all_gather(acts, SHARD, axis=0, tiled=True)

    proj = gather_axis(gather_axis(thrice(basis, acts, 1) * scale, "core"), "y")
    grads_t, proj = lax.optimization_barrier((grads.T.reshape(shards, cols, tok), proj))
    got = lax.all_to_all(grads_t, SHARD, 0, 0)
    got_t = got.transpose(1, 0, 2).reshape(cols, shards * tok)
    proj = gather_axis(proj, "z").reshape(shards, rank, tok).transpose(1, 0, 2).reshape(rank, shards * tok)
    base = thrice(basis, error_t, 1)

    factor = sum4(thrice(proj, got_t, 1) + base, "outer") / pods
    factor3 = jnp.concatenate(split3(factor), 0)
    keep, send = project(core.astype(jnp.int32).reshape(1), factor, factor3, got)
    inner = lax.all_to_all(keep + twin(send), ("z", "y"), 0, 0, tiled=True).sum(0)
    gram = inner[rank:, :rank]
    terms = thrice(inner[:rank] * scale, acts, 0) + thrice(factor, error_t, 0)
    rows = rank // 2
    mine = lax.dynamic_slice_in_dim(terms, core * rows, rows, 0)
    other = lax.dynamic_slice_in_dim(terms, (1 - core) * rows, rows, 0)
    tiles = (rows // 8, 8, width // 128, 128)
    mine = (mine + twin(other)).reshape(tiles).transpose(0, 2, 1, 3).reshape(chips, -1, 128)
    piece = lax.all_to_all(mine, CHIPS, 0, 0, tiled=True).sum(0) / pods
    mine = lax.all_to_all(jnp.broadcast_to(piece[None], mine.shape), CHIPS, 0, 0, tiled=True)
    other = twin(mine)
    terms = jnp.concatenate([jnp.where(core == 0, mine, other), jnp.where(core == 0, other, mine)], 0)
    terms = terms.reshape(rank // 8, width // 128, 8, 128).transpose(0, 2, 1, 3).reshape(rank, width)

    lower = jnp.linalg.cholesky(gram)
    inverse = jax.scipy.linalg.solve_triangular(lower, jnp.eye(rank, dtype=jnp.float32), lower=True)
    ortho = jnp.dot(inverse, factor, precision=highest)
    basis_out = jnp.dot(inverse, terms, precision=highest)

    oh, om, ol = split3(ortho)
    bh, bm, bl = split3(basis_out)
    ortho6 = jnp.concatenate([oh, oh, om, oh, ol, om], 0).T
    basis6 = jnp.concatenate([bh, bm, bh, bl, bh, bm], 0)

    place = lax.axis_index("outer").astype(jnp.int32).reshape(1)
    state = adam(place, ortho6, basis6, weight.T, moment_one.T, moment_two.T)
    error_out = finish_error(got, gathered, error_t, ortho6, basis6, scale)
    return (basis_out, error_out.T[None], state[0].T, state[1].T, state[2].T)


def solution(mesh):
    devices = mesh.devices
    mesh = Mesh(devices.reshape(devices.shape[0], 4, 4, -1), ALL)
    tokens = P(ALL, None)
    state = P("outer", SHARD)
    errors = P("outer", None, SHARD)
    return jax.shard_map(
        per_device,
        mesh=mesh,
        in_specs=(tokens, tokens, P(), errors, state, state, state),
        out_specs=(P(), errors, state, state, state),
        check_vma=False,
    )
```

```python
import jax
import jax.numpy as jnp
from jax import lax
from jax.experimental import pallas as pl
from jax.experimental.pallas import tpu as pltpu
from jax.sharding import Mesh, PartitionSpec as P

beta_one = 0.9
beta_two = 0.95
learn_rate = 0.01
decay_rate = 0.1
adam_epsilon = 1e-08
first_fix = 1.0 - 0.9**8
second_fix = 1.0 - 0.95**8

SHARD = ("z", "y", "core")
ALL = ("outer", "z", "y", "core")
CHIPS = ("outer", "z", "y")
VMEM_LIMIT = 48 * 1024 * 1024


def split3(x):
    high = lax.reduce_precision(x, 8, 7)
    rest = x - high
    middle = lax.reduce_precision(rest, 8, 7)
    return [p.astype(jnp.bfloat16) for p in (high, middle, rest - middle)]


def dot(a, b, ca, cb):
    return lax.dot_general(a, b, (((ca,), (cb,)), ((), ())), preferred_element_type=jnp.float32)


def thrice(x, b, cb):
    r = x.shape[0]
    y = dot(jnp.concatenate(split3(x), 0), b, 1, cb)
    return y[:r] + y[r : 2 * r] + y[2 * r :]


def swap(x, axis, k):
    return lax.ppermute(x, axis, [(i, i ^ k) for i in range(lax.axis_size(axis))])


def twin(x):
    return swap(x, "core", 1)


def sum4(x, axis):
    a, b, c = swap(x, axis, 1), swap(x, axis, 2), swap(x, axis, 3)
    return (x + a) + (b + c)


def gather_axis(x, axis):
    n = lax.axis_size(axis)
    i = lax.axis_index(axis)
    x = jnp.stack([x] + [swap(x, axis, k) for k in range(1, n)])
    bit = 1
    while bit < n:
        y = x.reshape((n // (2 * bit), 2, bit) + x.shape[1:])
        x = jnp.where((i & bit) != 0, y[:, ::-1], y).reshape(x.shape)
        bit *= 2
    return x


def parts3(x):
    high = x.astype(jnp.bfloat16)
    rest = x - high.astype(jnp.float32)
    middle = rest.astype(jnp.bfloat16)
    return high, middle, (rest - middle.astype(jnp.float32)).astype(jnp.bfloat16)


def project(core, factor, factor3, got):
    shards, cols, tok = got.shape
    rank = factor.shape[0]
    chips = shards // 2
    step = min(4, chips)
    extra = rank * rank // tok

    def body(c, f_ref, f3_ref, g_ref, keep_ref, send_ref, gram_ref):
        own = c[0] == 0

        @pl.when(pl.program_id(0) == 0)
        def _():
            h, m, l = parts3(f_ref[...])
            gram = dot(h, l, 1, 1) + dot(l, h, 1, 1) + dot(m, m, 1, 1)
            gram = gram + (dot(h, m, 1, 1) + dot(m, h, 1, 1)) + dot(h, h, 1, 1)
            gram_ref[...] = jnp.concatenate([gram[i * extra : (i + 1) * extra] for i in range(rank // extra)], axis=1)

        for k in range(step):
            pair = jnp.concatenate([g_ref[2 * k], g_ref[2 * k + 1]], axis=1)
            y = jnp.dot(f3_ref[...], pair, preferred_element_type=jnp.float32)
            y = y[:rank] + y[rank : 2 * rank] + y[2 * rank :]
            first, second = y[:, :tok], y[:, tok:]
            keep_ref[k, :rank] = jnp.where(own, first, second)
            send_ref[k, :rank] = jnp.where(own, second, first)
            keep_ref[k, rank:] = gram_ref[...]
            send_ref[k, rank:] = gram_ref[...]

    block = pl.BlockSpec((step, rank + extra, tok), lambda n, c: (n, 0, 0))
    return pl.pallas_call(
        body,
        out_shape=[jax.ShapeDtypeStruct((chips, rank + extra, tok), jnp.float32)] * 2,
        grid_spec=pltpu.PrefetchScalarGridSpec(
            num_scalar_prefetch=1,
            grid=(chips // step,),
            in_specs=[
                pl.BlockSpec((rank, cols), lambda n, c: (0, 0)),
                pl.BlockSpec((3 * rank, cols), lambda n, c: (0, 0)),
                pl.BlockSpec((2 * step, cols, tok), lambda n, c: (n, 0, 0)),
            ],
            out_specs=[block, block],
            scratch_shapes=[pltpu.VMEM((extra, tok), jnp.float32)],
        ),
        compiler_params=pltpu.CompilerParams(vmem_limit_bytes=VMEM_LIMIT),
        cost_estimate=pl.CostEstimate(flops=6 * rank * cols * shards * tok, bytes_accessed=2 * shards * cols * tok, transcendentals=0),
    )(core, factor, factor3, got)


def finish_error(got, gathered, error_t, ortho6, basis6, scale):
    shards, cols, tok = got.shape
    tokens, width = gathered.shape
    block = min(1024, width)
    depth6 = ortho6.shape[1]

    def body(got_ref, acts_ref, error_ref, ortho_ref, basis_ref, out_ref, columns):
        @pl.when(pl.program_id(0) == 0)
        def _():
            for s in range(shards):
                columns[:, s * tok : (s + 1) * tok] = got_ref[s]

        gradient = jnp.dot(columns[...], acts_ref[...], preferred_element_type=jnp.float32)
        approx = jnp.dot(ortho_ref[...], basis_ref[...], preferred_element_type=jnp.float32)
        matrix = gradient * scale + error_ref[...].astype(jnp.float32)
        out_ref[...] = (matrix - approx).astype(jnp.bfloat16)

    wide = pl.BlockSpec((cols, block), lambda n: (0, n))
    return pl.pallas_call(
        body,
        out_shape=jax.ShapeDtypeStruct(error_t.shape, jnp.bfloat16),
        grid=(width // block,),
        in_specs=[
            pl.BlockSpec((shards, cols, tok), lambda n: (0, 0, 0)),
            pl.BlockSpec((tokens, block), lambda n: (0, n)),
            wide,
            pl.BlockSpec((cols, depth6), lambda n: (0, 0)),
            pl.BlockSpec((depth6, block), lambda n: (0, n)),
        ],
        out_specs=wide,
        scratch_shapes=[pltpu.VMEM((cols, tokens), got.dtype)],
        compiler_params=pltpu.CompilerParams(vmem_limit_bytes=VMEM_LIMIT),
        cost_estimate=pl.CostEstimate(
            flops=2 * cols * width * (tokens + depth6), bytes_accessed=2 * tokens * (width + cols) + 4 * cols * width, transcendentals=0
        ),
    )(got, gathered, error_t, ortho6, basis6)


def adam(place, ortho6, basis6, weight, moment_one, moment_two):
    cols, rows = weight.shape
    block = min(256, rows)
    steps = rows // block
    depth6 = ortho6.shape[1]

    def body(p, ortho_ref, basis_ref, w_ref, one_ref, two_ref, w_out, one_out, two_out):
        update = jnp.dot(ortho_ref[...], basis_ref[...], preferred_element_type=jnp.float32)
        one = beta_one * one_ref[...] + (1.0 - beta_one) * update
        two = beta_two * two_ref[...] + (1.0 - beta_two) * update * update
        step = one / first_fix / (jnp.sqrt(two / second_fix) + adam_epsilon)
        w_out[...] = w_ref[...] * (1.0 - learn_rate * decay_rate) - learn_rate * step
        one_out[...] = one
        two_out[...] = two

    own = pl.BlockSpec((cols, block), lambda n, p: (0, n))
    return pl.pallas_call(
        body,
        out_shape=[jax.ShapeDtypeStruct(weight.shape, jnp.float32)] * 3,
        grid_spec=pltpu.PrefetchScalarGridSpec(
            num_scalar_prefetch=1,
            grid=(steps,),
            in_specs=[
                pl.BlockSpec((cols, depth6), lambda n, p: (0, 0)),
                pl.BlockSpec((depth6, block), lambda n, p: (0, p[0] * steps + n)),
                own,
                own,
                own,
            ],
            out_specs=[own, own, own],
        ),
        compiler_params=pltpu.CompilerParams(vmem_limit_bytes=VMEM_LIMIT),
        cost_estimate=pl.CostEstimate(flops=2 * cols * rows * depth6, bytes_accessed=24 * cols * rows, transcendentals=cols * rows),
    )(place, ortho6, basis6, weight, moment_one, moment_two)


def per_device(acts, grads, basis, error_in, weight, moment_one, moment_two):
    highest = lax.Precision.HIGHEST
    shards = lax.axis_size(SHARD)
    chips = lax.axis_size(CHIPS)
    pods = lax.axis_size("outer")
    tok, width = acts.shape
    cols = error_in.shape[2]
    rank = basis.shape[0]
    scale = (tok * shards) ** (-0.5)
    core = lax.axis_index("core")
    error_t = error_in[0].T
    gathered = lax.all_gather(acts, SHARD, axis=0, tiled=True)

    proj = gather_axis(thrice(basis, acts, 1) * scale, "y")
    grads_t, proj = lax.optimization_barrier((grads.T.reshape(shards, cols, tok), proj))
    got = lax.all_to_all(grads_t, SHARD, 0, 0)
    got_t = got.transpose(1, 0, 2).reshape(cols, shards * tok)
    proj = gather_axis(gather_axis(proj, "z"), "core").transpose(3, 1, 2, 0, 4).reshape(rank, shards * tok)
    base = thrice(basis, error_t, 1)

    factor = sum4(thrice(proj, got_t, 1) + base, "outer") / pods
    factor3 = jnp.concatenate(split3(factor), 0)
    keep, send = project(core.astype(jnp.int32).reshape(1), factor, factor3, got)
    inner = lax.all_to_all(keep + twin(send), ("z", "y"), 0, 0, tiled=True).sum(0)
    gram = jnp.concatenate([inner[rank:, i : i + rank] for i in range(0, tok, rank)], 0)
    terms = thrice(inner[:rank] * scale, acts, 0) + thrice(factor, error_t, 0)
    rows = rank // 2
    mine = lax.dynamic_slice_in_dim(terms, core * rows, rows, 0)
    other = lax.dynamic_slice_in_dim(terms, (1 - core) * rows, rows, 0)
    tiles = (rows // 8, 8, width // 128, 128)
    mine = (mine + twin(other)).reshape(tiles).transpose(0, 2, 1, 3).reshape(chips, -1, 128)
    piece = lax.all_to_all(mine, CHIPS, 0, 0, tiled=True).sum(0) / pods
    mine = lax.all_to_all(jnp.broadcast_to(piece[None], mine.shape), CHIPS, 0, 0, tiled=True)
    other = twin(mine)
    terms = jnp.concatenate([jnp.where(core == 0, mine, other), jnp.where(core == 0, other, mine)], 0)
    terms = terms.reshape(rank // 8, width // 128, 8, 128).transpose(0, 2, 1, 3).reshape(rank, width)

    lower = jnp.linalg.cholesky(gram)
    inverse = jax.scipy.linalg.solve_triangular(lower, jnp.eye(rank, dtype=jnp.float32), lower=True)
    ortho = jnp.dot(inverse, factor, precision=highest)
    basis_out = jnp.dot(inverse, terms, precision=highest)

    oh, om, ol = split3(ortho)
    bh, bm, bl = split3(basis_out)
    ortho6 = jnp.concatenate([oh, oh, om, oh, ol, om], 0).T
    basis6 = jnp.concatenate([bh, bm, bh, bl, bh, bm], 0)

    place = lax.axis_index("outer").astype(jnp.int32).reshape(1)
    state = adam(place, ortho6, basis6, weight.T, moment_one.T, moment_two.T)
    error_out = finish_error(got, gathered, error_t, ortho6, basis6, scale)
    return (basis_out, error_out.T[None], state[0].T, state[1].T, state[2].T)


def solution(mesh):
    devices = mesh.devices
    mesh = Mesh(devices.reshape(devices.shape[0], 4, 4, -1), ALL)
    tokens = P(ALL, None)
    state = P("outer", SHARD)
    errors = P("outer", None, SHARD)
    return jax.shard_map(
        per_device,
        mesh=mesh,
        in_specs=(tokens, tokens, P(), errors, state, state, state),
        out_specs=(P(), errors, state, state, state),
        check_vma=False,
    )
```

```python
import jax
import jax.numpy as jnp
from jax import lax
from jax.experimental import pallas as pl
from jax.experimental.pallas import tpu as pltpu
from jax.sharding import Mesh, PartitionSpec as P

beta_one = 0.9
beta_two = 0.95
learn_rate = 0.01
decay_rate = 0.1
adam_epsilon = 1e-08
first_fix = 1.0 - 0.9**8
second_fix = 1.0 - 0.95**8

SHARD = ("z", "y", "core")
ALL = ("outer", "z", "y", "core")
CHIPS = ("outer", "z", "y")
VMEM_LIMIT = 48 * 1024 * 1024


def split3(x):
    high = lax.reduce_precision(x, 8, 7)
    rest = x - high
    middle = lax.reduce_precision(rest, 8, 7)
    return [p.astype(jnp.bfloat16) for p in (high, middle, rest - middle)]


def dot(a, b, ca, cb):
    return lax.dot_general(a, b, (((ca,), (cb,)), ((), ())), preferred_element_type=jnp.float32)


def thrice(x, b, cb):
    r = x.shape[0]
    y = dot(jnp.concatenate(split3(x), 0), b, 1, cb)
    return y[:r] + y[r : 2 * r] + y[2 * r :]


def swap(x, axis, k):
    return lax.ppermute(x, axis, [(i, i ^ k) for i in range(lax.axis_size(axis))])


def twin(x):
    return swap(x, "core", 1)


def sum4(x, axis):
    a, b, c = swap(x, axis, 1), swap(x, axis, 2), swap(x, axis, 3)
    return (x + a) + (b + c)


def scatter4(x, axis):
    i = lax.axis_index(axis)
    own, a, b, c = (lax.dynamic_index_in_dim(x, i ^ k, 0, keepdims=False) for k in range(4))
    a, b, c = (swap(v, axis, k) for v, k in ((a, 1), (b, 2), (c, 3)))
    return (own + a) + (b + c)


def gather_axis(x, axis):
    n = lax.axis_size(axis)
    i = lax.axis_index(axis)
    x = jnp.stack([x] + [swap(x, axis, k) for k in range(1, n)])
    bit = 1
    while bit < n:
        y = x.reshape((n // (2 * bit), 2, bit) + x.shape[1:])
        x = jnp.where((i & bit) != 0, y[:, ::-1], y).reshape(x.shape)
        bit *= 2
    return x


def parts3(x):
    high = x.astype(jnp.bfloat16)
    rest = x - high.astype(jnp.float32)
    middle = rest.astype(jnp.bfloat16)
    return high, middle, (rest - middle.astype(jnp.float32)).astype(jnp.bfloat16)


def project(core, factor, factor3, got):
    shards, cols, tok = got.shape
    rank = factor.shape[0]
    chips = shards // 2
    step = min(4, chips)
    extra = rank * rank // tok

    def body(c, f_ref, f3_ref, g_ref, keep_ref, send_ref, gram_ref):
        own = c[0] == 0

        @pl.when(pl.program_id(0) == 0)
        def _():
            h, m, l = parts3(f_ref[...])
            gram = dot(h, l, 1, 1) + dot(l, h, 1, 1) + dot(m, m, 1, 1)
            gram = gram + (dot(h, m, 1, 1) + dot(m, h, 1, 1)) + dot(h, h, 1, 1)
            gram_ref[...] = jnp.concatenate([gram[i * extra : (i + 1) * extra] for i in range(rank // extra)], axis=1)

        for k in range(step):
            pair = jnp.concatenate([g_ref[2 * k], g_ref[2 * k + 1]], axis=1)
            y = jnp.dot(f3_ref[...], pair, preferred_element_type=jnp.float32)
            y = y[:rank] + y[rank : 2 * rank] + y[2 * rank :]
            first, second = y[:, :tok], y[:, tok:]
            keep_ref[k, :rank] = jnp.where(own, first, second)
            send_ref[k, :rank] = jnp.where(own, second, first)
            keep_ref[k, rank:] = gram_ref[...]
            send_ref[k, rank:] = gram_ref[...]

    block = pl.BlockSpec((step, rank + extra, tok), lambda n, c: (n, 0, 0))
    return pl.pallas_call(
        body,
        out_shape=[jax.ShapeDtypeStruct((chips, rank + extra, tok), jnp.float32)] * 2,
        grid_spec=pltpu.PrefetchScalarGridSpec(
            num_scalar_prefetch=1,
            grid=(chips // step,),
            in_specs=[
                pl.BlockSpec((rank, cols), lambda n, c: (0, 0)),
                pl.BlockSpec((3 * rank, cols), lambda n, c: (0, 0)),
                pl.BlockSpec((2 * step, cols, tok), lambda n, c: (n, 0, 0)),
            ],
            out_specs=[block, block],
            scratch_shapes=[pltpu.VMEM((extra, tok), jnp.float32)],
        ),
        compiler_params=pltpu.CompilerParams(vmem_limit_bytes=VMEM_LIMIT),
        cost_estimate=pl.CostEstimate(flops=6 * rank * cols * shards * tok, bytes_accessed=2 * shards * cols * tok, transcendentals=0),
    )(core, factor, factor3, got)


def finish_error(got, gathered, error_t, ortho6, basis6, scale):
    shards, cols, tok = got.shape
    tokens, width = gathered.shape
    block = min(1024, width)
    steps = width // block
    depth6 = ortho6.shape[1]
    parts = 4
    rows = tokens // parts

    def body(got_ref, acts_ref, error_ref, ortho_ref, basis_ref, out_ref, columns, held, gradient, sems):
        n = pl.program_id(0)
        slot = lax.rem(n, 2)

        def copy(m, s, k):
            piece = pl.ds(k * rows, rows)
            place = pl.ds(pl.multiple_of(m * block, block), block)
            return pltpu.make_async_copy(acts_ref.at[piece, place], held.at[s, piece], sems.at[s, k])

        @pl.when(n == 0)
        def _():
            for k in range(parts):
                copy(0, 0, k).start()
            if steps > 1:
                for k in range(parts):
                    copy(1, 1, k).start()
            for s in range(shards):
                columns[:, s * tok : (s + 1) * tok] = got_ref[s]
            total = None
            for k in range(parts):
                copy(0, 0, k).wait()
                piece = slice(k * rows, (k + 1) * rows)
                d = jnp.dot(columns[:, piece], held[0, piece], preferred_element_type=jnp.float32)
                total = d if total is None else total + d
            gradient[...] = total

        @pl.when(n > 0)
        def _():
            for k in range(parts):
                copy(n, slot, k).wait()
            gradient[...] = jnp.dot(columns[...], held[slot], preferred_element_type=jnp.float32)

        @pl.when(n + 2 < steps)
        def _():
            for k in range(parts):
                copy(n + 2, slot, k).start()

        approx = jnp.dot(ortho_ref[...], basis_ref[...], preferred_element_type=jnp.float32)
        matrix = gradient[...] * scale + error_ref[...].astype(jnp.float32)
        out_ref[...] = (matrix - approx).astype(jnp.bfloat16)

    wide = pl.BlockSpec((cols, block), lambda n: (0, n))
    return pl.pallas_call(
        body,
        out_shape=jax.ShapeDtypeStruct(error_t.shape, jnp.bfloat16),
        grid=(steps,),
        in_specs=[
            pl.BlockSpec((shards, cols, tok), lambda n: (0, 0, 0)),
            pl.BlockSpec(memory_space=pl.ANY),
            wide,
            pl.BlockSpec((cols, depth6), lambda n: (0, 0)),
            pl.BlockSpec((depth6, block), lambda n: (0, n)),
        ],
        out_specs=wide,
        scratch_shapes=[
            pltpu.VMEM((cols, tokens), got.dtype),
            pltpu.VMEM((2, tokens, block), gathered.dtype),
            pltpu.VMEM((cols, block), jnp.float32),
            pltpu.SemaphoreType.DMA((2, parts)),
        ],
        compiler_params=pltpu.CompilerParams(vmem_limit_bytes=VMEM_LIMIT),
        cost_estimate=pl.CostEstimate(
            flops=2 * cols * width * (tokens + depth6), bytes_accessed=2 * tokens * (width + cols) + 4 * cols * width, transcendentals=0
        ),
    )(got, gathered, error_t, ortho6, basis6)


def adam(place, ortho6, basis6, weight, moment_one, moment_two):
    cols, rows = weight.shape
    block = min(256, rows)
    steps = rows // block
    depth6 = ortho6.shape[1]

    def body(p, ortho_ref, basis_ref, w_ref, one_ref, two_ref, w_out, one_out, two_out):
        update = jnp.dot(ortho_ref[...], basis_ref[...], preferred_element_type=jnp.float32)
        one = beta_one * one_ref[...] + (1.0 - beta_one) * update
        two = beta_two * two_ref[...] + (1.0 - beta_two) * update * update
        root = jnp.sqrt(two * (1.0 / second_fix)) + adam_epsilon
        step = one * (learn_rate / first_fix) / root
        w_out[...] = w_ref[...] * (1.0 - learn_rate * decay_rate) - step
        one_out[...] = one
        two_out[...] = two

    own = pl.BlockSpec((cols, block), lambda n, p: (0, n))
    return pl.pallas_call(
        body,
        out_shape=[jax.ShapeDtypeStruct(weight.shape, jnp.float32)] * 3,
        grid_spec=pltpu.PrefetchScalarGridSpec(
            num_scalar_prefetch=1,
            grid=(steps,),
            in_specs=[
                pl.BlockSpec((cols, depth6), lambda n, p: (0, 0)),
                pl.BlockSpec((depth6, block), lambda n, p: (0, p[0] * steps + n)),
                own,
                own,
                own,
            ],
            out_specs=[own, own, own],
        ),
        compiler_params=pltpu.CompilerParams(vmem_limit_bytes=VMEM_LIMIT),
        cost_estimate=pl.CostEstimate(flops=2 * cols * rows * depth6, bytes_accessed=24 * cols * rows, transcendentals=cols * rows),
    )(place, ortho6, basis6, weight, moment_one, moment_two)


def per_device(acts, grads, basis, error_in, weight, moment_one, moment_two):
    highest = lax.Precision.HIGHEST
    shards = lax.axis_size(SHARD)
    chips = lax.axis_size(CHIPS)
    pods = lax.axis_size("outer")
    tok, width = acts.shape
    cols = error_in.shape[2]
    rank = basis.shape[0]
    scale = (tok * shards) ** (-0.5)
    core = lax.axis_index("core")
    error_t = error_in[0].T
    gathered = lax.all_gather(acts, SHARD, axis=0, tiled=True)

    proj = gather_axis(thrice(basis, acts, 1) * scale, "y")
    grads_t, proj = lax.optimization_barrier((grads.T.reshape(shards, cols, tok), proj))
    got = lax.all_to_all(grads_t, SHARD, 0, 0)
    got_t = got.transpose(1, 0, 2).reshape(cols, shards * tok)
    base = thrice(basis, error_t, 1)
    proj, base = lax.optimization_barrier((gather_axis(proj, "z"), base))
    other = twin(proj)
    proj = jnp.stack([jnp.where(core == 0, proj, other), jnp.where(core == 0, other, proj)], 2)
    proj = proj.transpose(3, 0, 1, 2, 4).reshape(rank, shards * tok)

    factor = sum4(thrice(proj, got_t, 1) + base, "outer") / pods
    factor3 = jnp.concatenate(split3(factor), 0)
    keep, send = project(core.astype(jnp.int32).reshape(1), factor, factor3, got)
    inner = lax.all_to_all(keep + twin(send), ("z", "y"), 0, 0, tiled=True).sum(0)
    gram = jnp.concatenate([inner[rank:, i : i + rank] for i in range(0, tok, rank)], 0)
    terms = thrice(inner[:rank] * scale, acts, 0) + thrice(factor, error_t, 0)

    half = width // 2
    mine = lax.dynamic_slice_in_dim(terms, core * half, half, 1)
    other = lax.dynamic_slice_in_dim(terms, (1 - core) * half, half, 1)
    mine = scatter4((mine + twin(other)).reshape(pods, rank // pods, half), "outer")
    mine, gram = lax.optimization_barrier((mine, gram))
    mine = mine.reshape(rank // pods, chips // pods, -1).transpose(1, 0, 2)
    piece = lax.all_to_all(mine, ("z", "y"), 0, 0, tiled=True).sum(0) / pods
    mine = lax.all_to_all(jnp.broadcast_to(piece[None], (chips,) + piece.shape), CHIPS, 0, 0, tiled=True)
    mine = mine.reshape((pods, chips // pods) + piece.shape)
    other = twin(mine)
    terms = jnp.concatenate([jnp.where(core == 0, mine, other), jnp.where(core == 0, other, mine)], 1)
    terms = terms.transpose(0, 2, 1, 3).reshape(rank, width)

    lower = jnp.linalg.cholesky(gram)
    inverse = jax.scipy.linalg.solve_triangular(lower, jnp.eye(rank, dtype=jnp.float32), lower=True)
    ortho = jnp.dot(inverse, factor, precision=highest)
    basis_out = jnp.dot(inverse, terms, precision=highest)

    oh, om, ol = split3(ortho)
    bh, bm, bl = split3(basis_out)
    ortho6 = jnp.concatenate([oh, oh, om, oh, ol, om], 0).T
    basis6 = jnp.concatenate([bh, bm, bh, bl, bh, bm], 0)

    place = lax.axis_index("outer").astype(jnp.int32).reshape(1)
    state = adam(place, ortho6, basis6, weight.T, moment_one.T, moment_two.T)
    error_out = finish_error(got, gathered, error_t, ortho6, basis6, scale)
    return (basis_out, error_out.T[None], state[0].T, state[1].T, state[2].T)


def solution(mesh):
    devices = mesh.devices
    mesh = Mesh(devices.reshape(devices.shape[0], 4, 4, -1), ALL)
    tokens = P(ALL, None)
    state = P("outer", SHARD)
    errors = P("outer", None, SHARD)
    return jax.shard_map(
        per_device,
        mesh=mesh,
        in_specs=(tokens, tokens, P(), errors, state, state, state),
        out_specs=(P(), errors, state, state, state),
        check_vma=False,
    )
```

```python
import jax
import jax.numpy as jnp
from jax import lax
from jax.experimental import pallas as pl
from jax.experimental.pallas import tpu as pltpu
from jax.sharding import Mesh, PartitionSpec as P

beta_one = 0.9
beta_two = 0.95
learn_rate = 0.01
decay_rate = 0.1
adam_epsilon = 1e-08
first_fix = 1.0 - 0.9**8
second_fix = 1.0 - 0.95**8

SHARD = ("z", "y", "core")
ALL = ("outer", "z", "y", "core")
CHIPS = ("outer", "z", "y")
VMEM_LIMIT = 48 * 1024 * 1024


def split3(x):
    high = lax.reduce_precision(x, 8, 7)
    rest = x - high
    middle = lax.reduce_precision(rest, 8, 7)
    return [p.astype(jnp.bfloat16) for p in (high, middle, rest - middle)]


def dot(a, b, ca, cb):
    return lax.dot_general(a, b, (((ca,), (cb,)), ((), ())), preferred_element_type=jnp.float32)


def thrice(x, b, cb):
    r = x.shape[0]
    y = dot(jnp.concatenate(split3(x), 0), b, 1, cb)
    return y[:r] + y[r : 2 * r] + y[2 * r :]


def swap(x, axis, k):
    return lax.ppermute(x, axis, [(i, i ^ k) for i in range(lax.axis_size(axis))])


def twin(x):
    return swap(x, "core", 1)


def sum4(x, axis):
    a, b, c = swap(x, axis, 1), swap(x, axis, 2), swap(x, axis, 3)
    return (x + a) + (b + c)


def scatter4(x, axis):
    i = lax.axis_index(axis)
    own, a, b, c = (lax.dynamic_index_in_dim(x, i ^ k, 0, keepdims=False) for k in range(4))
    a, b, c = (swap(v, axis, k) for v, k in ((a, 1), (b, 2), (c, 3)))
    return (own + a) + (b + c)


def gather_axis(x, axis):
    n = lax.axis_size(axis)
    i = lax.axis_index(axis)
    x = jnp.stack([x] + [swap(x, axis, k) for k in range(1, n)])
    bit = 1
    while bit < n:
        y = x.reshape((n // (2 * bit), 2, bit) + x.shape[1:])
        x = jnp.where((i & bit) != 0, y[:, ::-1], y).reshape(x.shape)
        bit *= 2
    return x


def parts3(x):
    high = x.astype(jnp.bfloat16)
    rest = x - high.astype(jnp.float32)
    middle = rest.astype(jnp.bfloat16)
    return high, middle, (rest - middle.astype(jnp.float32)).astype(jnp.bfloat16)


def project(core, factor, factor3, got):
    shards, cols, tok = got.shape
    rank = factor.shape[0]
    chips = shards // 2
    step = min(8, chips)
    extra = rank * rank // tok

    def body(c, f_ref, f3_ref, g_ref, keep_ref, send_ref, gram_ref):
        own = c[0] == 0

        @pl.when(pl.program_id(0) == 0)
        def _():
            h, m, l = parts3(f_ref[...])
            gram = dot(h, l, 1, 1) + dot(l, h, 1, 1) + dot(m, m, 1, 1)
            gram = gram + (dot(h, m, 1, 1) + dot(m, h, 1, 1)) + dot(h, h, 1, 1)
            gram_ref[...] = jnp.concatenate([gram[i * extra : (i + 1) * extra] for i in range(rank // extra)], axis=1)

        for k in range(step):
            pair = jnp.concatenate([g_ref[2 * k], g_ref[2 * k + 1]], axis=1)
            y = jnp.dot(f3_ref[...], pair, preferred_element_type=jnp.float32)
            y = y[:rank] + y[rank : 2 * rank] + y[2 * rank :]
            first, second = y[:, :tok], y[:, tok:]
            keep_ref[k, :rank] = jnp.where(own, first, second)
            send_ref[k, :rank] = jnp.where(own, second, first)
            keep_ref[k, rank:] = gram_ref[...]
            send_ref[k, rank:] = gram_ref[...]

    block = pl.BlockSpec((step, rank + extra, tok), lambda n, c: (n, 0, 0))
    return pl.pallas_call(
        body,
        out_shape=[jax.ShapeDtypeStruct((chips, rank + extra, tok), jnp.float32)] * 2,
        grid_spec=pltpu.PrefetchScalarGridSpec(
            num_scalar_prefetch=1,
            grid=(chips // step,),
            in_specs=[
                pl.BlockSpec((rank, cols), lambda n, c: (0, 0)),
                pl.BlockSpec((3 * rank, cols), lambda n, c: (0, 0)),
                pl.BlockSpec((2 * step, cols, tok), lambda n, c: (n, 0, 0)),
            ],
            out_specs=[block, block],
            scratch_shapes=[pltpu.VMEM((extra, tok), jnp.float32)],
        ),
        compiler_params=pltpu.CompilerParams(vmem_limit_bytes=VMEM_LIMIT),
        cost_estimate=pl.CostEstimate(flops=6 * rank * cols * shards * tok, bytes_accessed=2 * shards * cols * tok, transcendentals=0),
    )(core, factor, factor3, got)


def finish_error(got, gathered, error_t, ortho6, basis6, scale):
    shards, cols, tok = got.shape
    tokens, width = gathered.shape
    block = min(1024, width)
    steps = width // block
    depth6 = ortho6.shape[1]
    parts = 8
    rows = tokens // parts

    def body(got_ref, acts_ref, error_ref, ortho_ref, basis_ref, out_ref, columns, held, sems):
        n = pl.program_id(0)
        slot = lax.rem(n, 2)

        def copy(m, s, k):
            piece = pl.ds(k * rows, rows)
            place = pl.ds(pl.multiple_of(m * block, block), block)
            return pltpu.make_async_copy(acts_ref.at[piece, place], held.at[s, piece], sems.at[s, k])

        def close(gradient):
            approx = jnp.dot(ortho_ref[...], basis_ref[...], preferred_element_type=jnp.float32)
            matrix = gradient * scale + error_ref[...].astype(jnp.float32)
            out_ref[...] = (matrix - approx).astype(jnp.bfloat16)

        @pl.when(n == 0)
        def _():
            for k in range(parts):
                copy(0, 0, k).start()
            if steps > 1:
                for k in range(parts):
                    copy(1, 1, k).start()
            for s in range(shards):
                columns[:, s * tok : (s + 1) * tok] = got_ref[s]
            total = None
            for k in range(parts):
                copy(0, 0, k).wait()
                piece = slice(k * rows, (k + 1) * rows)
                d = jnp.dot(columns[:, piece], held[0, piece], preferred_element_type=jnp.float32)
                total = d if total is None else total + d
            close(total)

        @pl.when(n > 0)
        def _():
            for k in range(parts):
                copy(n, slot, k).wait()
            close(jnp.dot(columns[...], held[slot], preferred_element_type=jnp.float32))

        @pl.when(n + 2 < steps)
        def _():
            for k in range(parts):
                copy(n + 2, slot, k).start()

    wide = pl.BlockSpec((cols, block), lambda n: (0, n))
    return pl.pallas_call(
        body,
        out_shape=jax.ShapeDtypeStruct(error_t.shape, jnp.bfloat16),
        grid=(steps,),
        in_specs=[
            pl.BlockSpec((shards, cols, tok), lambda n: (0, 0, 0)),
            pl.BlockSpec(memory_space=pl.ANY),
            wide,
            pl.BlockSpec((cols, depth6), lambda n: (0, 0)),
            pl.BlockSpec((depth6, block), lambda n: (0, n)),
        ],
        out_specs=wide,
        scratch_shapes=[
            pltpu.VMEM((cols, tokens), got.dtype),
            pltpu.VMEM((2, tokens, block), gathered.dtype),
            pltpu.SemaphoreType.DMA((2, parts)),
        ],
        compiler_params=pltpu.CompilerParams(vmem_limit_bytes=VMEM_LIMIT),
        cost_estimate=pl.CostEstimate(
            flops=2 * cols * width * (tokens + depth6), bytes_accessed=2 * tokens * (width + cols) + 4 * cols * width, transcendentals=0
        ),
    )(got, gathered, error_t, ortho6, basis6)


def adam(place, ortho6, basis6, weight, moment_one, moment_two):
    cols, rows = weight.shape
    block = min(512, rows)
    steps = rows // block
    depth6 = ortho6.shape[1]

    def body(p, ortho_ref, basis_ref, w_ref, one_ref, two_ref, w_out, one_out, two_out):
        update = jnp.dot(ortho_ref[...], basis_ref[...], preferred_element_type=jnp.float32)
        one = beta_one * one_ref[...] + (1.0 - beta_one) * update
        two = beta_two * two_ref[...] + (1.0 - beta_two) * update * update
        root = jnp.sqrt(two * (1.0 / second_fix)) + adam_epsilon
        step = one * (learn_rate / first_fix) / root
        w_out[...] = w_ref[...] * (1.0 - learn_rate * decay_rate) - step
        one_out[...] = one
        two_out[...] = two

    own = pl.BlockSpec((cols, block), lambda n, p: (0, n))
    return pl.pallas_call(
        body,
        out_shape=[jax.ShapeDtypeStruct(weight.shape, jnp.float32)] * 3,
        grid_spec=pltpu.PrefetchScalarGridSpec(
            num_scalar_prefetch=1,
            grid=(steps,),
            in_specs=[
                pl.BlockSpec((cols, depth6), lambda n, p: (0, 0)),
                pl.BlockSpec((depth6, block), lambda n, p: (0, p[0] * steps + n)),
                own,
                own,
                own,
            ],
            out_specs=[own, own, own],
        ),
        compiler_params=pltpu.CompilerParams(vmem_limit_bytes=VMEM_LIMIT),
        cost_estimate=pl.CostEstimate(flops=2 * cols * rows * depth6, bytes_accessed=24 * cols * rows, transcendentals=cols * rows),
    )(place, ortho6, basis6, weight, moment_one, moment_two)


def per_device(acts, grads, basis, error_in, weight, moment_one, moment_two):
    highest = lax.Precision.HIGHEST
    shards = lax.axis_size(SHARD)
    chips = lax.axis_size(CHIPS)
    pods = lax.axis_size("outer")
    tok, width = acts.shape
    cols = error_in.shape[2]
    rank = basis.shape[0]
    scale = (tok * shards) ** (-0.5)
    core = lax.axis_index("core")
    error_t = error_in[0].T
    gathered = lax.all_gather(acts, SHARD, axis=0, tiled=True)

    proj = gather_axis(thrice(basis, acts, 1) * scale, "y")
    grads_t, proj = lax.optimization_barrier((grads.T.reshape(shards, cols, tok), proj))
    got = lax.all_to_all(grads_t, SHARD, 0, 0)
    got_t = got.transpose(1, 0, 2).reshape(cols, shards * tok)
    base = thrice(basis, error_t, 1)
    proj, base = lax.optimization_barrier((gather_axis(proj, "z"), base))
    other = twin(proj)
    proj = jnp.stack([jnp.where(core == 0, proj, other), jnp.where(core == 0, other, proj)], 2)
    proj = proj.transpose(3, 0, 1, 2, 4).reshape(rank, shards * tok)

    factor = sum4(thrice(proj, got_t, 1) + base, "outer") / pods
    factor3 = jnp.concatenate(split3(factor), 0)
    keep, send = project(core.astype(jnp.int32).reshape(1), factor, factor3, got)
    inner = lax.all_to_all(keep + twin(send), ("z", "y"), 0, 0, tiled=True).sum(0)
    gram = jnp.concatenate([inner[rank:, i : i + rank] for i in range(0, tok, rank)], 0)
    terms = thrice(inner[:rank] * scale, acts, 0) + thrice(factor, error_t, 0)

    half = width // 2
    mine = lax.dynamic_slice_in_dim(terms, core * half, half, 1)
    other = lax.dynamic_slice_in_dim(terms, (1 - core) * half, half, 1)
    mine = scatter4((mine + twin(other)).reshape(pods, rank // pods, half), "outer")
    mine, gram = lax.optimization_barrier((mine, gram))
    mine = mine.reshape(rank // pods, chips // pods, -1).transpose(1, 0, 2)
    piece = lax.all_to_all(mine, ("z", "y"), 0, 0, tiled=True).sum(0) / pods
    mine = lax.all_to_all(jnp.broadcast_to(piece[None], (chips,) + piece.shape), CHIPS, 0, 0, tiled=True)
    mine = mine.reshape((pods, chips // pods) + piece.shape)
    other = twin(mine)
    terms = jnp.concatenate([jnp.where(core == 0, mine, other), jnp.where(core == 0, other, mine)], 1)
    terms = terms.transpose(0, 2, 1, 3).reshape(rank, width)

    lower = jnp.linalg.cholesky(gram)
    inverse = jax.scipy.linalg.solve_triangular(lower, jnp.eye(rank, dtype=jnp.float32), lower=True)
    ortho = jnp.dot(inverse, factor, precision=highest)
    basis_out = jnp.dot(inverse, terms, precision=highest)

    oh, om, ol = split3(ortho)
    bh, bm, bl = split3(basis_out)
    ortho6 = jnp.concatenate([oh, oh, om, oh, ol, om], 0).T
    basis6 = jnp.concatenate([bh, bm, bh, bl, bh, bm], 0)

    place = lax.axis_index("outer").astype(jnp.int32).reshape(1)
    state = adam(place, ortho6, basis6, weight.T, moment_one.T, moment_two.T)
    error_out = finish_error(got, gathered, error_t, ortho6, basis6, scale)
    return (basis_out, error_out.T[None], state[0].T, state[1].T, state[2].T)


def solution(mesh):
    devices = mesh.devices
    mesh = Mesh(devices.reshape(devices.shape[0], 4, 4, -1), ALL)
    tokens = P(ALL, None)
    state = P("outer", SHARD)
    errors = P("outer", None, SHARD)
    return jax.shard_map(
        per_device,
        mesh=mesh,
        in_specs=(tokens, tokens, P(), errors, state, state, state),
        out_specs=(P(), errors, state, state, state),
        check_vma=False,
    )
```

```python
import jax
import jax.numpy as jnp
from jax import lax
from jax.experimental import pallas as pl
from jax.experimental.pallas import tpu as pltpu
from jax.sharding import Mesh, PartitionSpec as P

beta_one = 0.9
beta_two = 0.95
learn_rate = 0.01
decay_rate = 0.1
adam_epsilon = 1e-08
first_fix = 1.0 - 0.9**8
second_fix = 1.0 - 0.95**8

SHARD = ("z", "y", "core")
ALL = ("outer", "z", "y", "core")
CHIPS = ("outer", "z", "y")
VMEM_LIMIT = 48 * 1024 * 1024


def split3(x):
    high = lax.reduce_precision(x, 8, 7)
    rest = x - high
    middle = lax.reduce_precision(rest, 8, 7)
    return [p.astype(jnp.bfloat16) for p in (high, middle, rest - middle)]


def dot(a, b, ca, cb):
    return lax.dot_general(a, b, (((ca,), (cb,)), ((), ())), preferred_element_type=jnp.float32)


def thrice(x, b, cb):
    r = x.shape[0]
    y = dot(jnp.concatenate(split3(x), 0), b, 1, cb)
    return y[:r] + y[r : 2 * r] + y[2 * r :]


def swap(x, axis, k):
    return lax.ppermute(x, axis, [(i, i ^ k) for i in range(lax.axis_size(axis))])


def twin(x):
    return swap(x, "core", 1)


def sum4(x, axis):
    a, b, c = swap(x, axis, 1), swap(x, axis, 2), swap(x, axis, 3)
    return (x + a) + (b + c)


def scatter4(x, axis):
    i = lax.axis_index(axis)
    own, a, b, c = (lax.dynamic_index_in_dim(x, i ^ k, 0, keepdims=False) for k in range(4))
    a, b, c = (swap(v, axis, k) for v, k in ((a, 1), (b, 2), (c, 3)))
    return (own + a) + (b + c)


def gather_axis(x, axis):
    n = lax.axis_size(axis)
    i = lax.axis_index(axis)
    x = jnp.stack([x] + [swap(x, axis, k) for k in range(1, n)])
    bit = 1
    while bit < n:
        y = x.reshape((n // (2 * bit), 2, bit) + x.shape[1:])
        x = jnp.where((i & bit) != 0, y[:, ::-1], y).reshape(x.shape)
        bit *= 2
    return x


def parts3(x):
    high = x.astype(jnp.bfloat16)
    rest = x - high.astype(jnp.float32)
    middle = rest.astype(jnp.bfloat16)
    return high, middle, (rest - middle.astype(jnp.float32)).astype(jnp.bfloat16)


def project(core, factor, factor3, got):
    shards, cols, tok = got.shape
    rank = factor.shape[0]
    chips = shards // 2
    step = min(8, chips)
    extra = rank * rank // tok

    def body(c, f_ref, f3_ref, g_ref, keep_ref, send_ref, gram_ref):
        own = c[0] == 0

        @pl.when(pl.program_id(0) == 0)
        def _():
            h, m, l = parts3(f_ref[...])
            gram = dot(h, l, 1, 1) + dot(l, h, 1, 1) + dot(m, m, 1, 1)
            gram = gram + (dot(h, m, 1, 1) + dot(m, h, 1, 1)) + dot(h, h, 1, 1)
            gram_ref[...] = jnp.concatenate([gram[i * extra : (i + 1) * extra] for i in range(rank // extra)], axis=1)

        for k in range(step):
            pair = jnp.concatenate([g_ref[2 * k], g_ref[2 * k + 1]], axis=1)
            y = jnp.dot(f3_ref[...], pair, preferred_element_type=jnp.float32)
            y = y[:rank] + y[rank : 2 * rank] + y[2 * rank :]
            first, second = y[:, :tok], y[:, tok:]
            keep_ref[k, :rank] = jnp.where(own, first, second)
            send_ref[k, :rank] = jnp.where(own, second, first)
            keep_ref[k, rank:] = gram_ref[...]
            send_ref[k, rank:] = gram_ref[...]

    block = pl.BlockSpec((step, rank + extra, tok), lambda n, c: (n, 0, 0))
    return pl.pallas_call(
        body,
        out_shape=[jax.ShapeDtypeStruct((chips, rank + extra, tok), jnp.float32)] * 2,
        grid_spec=pltpu.PrefetchScalarGridSpec(
            num_scalar_prefetch=1,
            grid=(chips // step,),
            in_specs=[
                pl.BlockSpec((rank, cols), lambda n, c: (0, 0)),
                pl.BlockSpec((3 * rank, cols), lambda n, c: (0, 0)),
                pl.BlockSpec((2 * step, cols, tok), lambda n, c: (n, 0, 0)),
            ],
            out_specs=[block, block],
            scratch_shapes=[pltpu.VMEM((extra, tok), jnp.float32)],
        ),
        compiler_params=pltpu.CompilerParams(vmem_limit_bytes=VMEM_LIMIT),
        cost_estimate=pl.CostEstimate(flops=6 * rank * cols * shards * tok, bytes_accessed=2 * shards * cols * tok, transcendentals=0),
    )(core, factor, factor3, got)


def finish_error(got, gathered, error_t, ortho6, basis6, scale):
    shards, cols, tok = got.shape
    tokens, width = gathered.shape
    block = min(1024, width)
    steps = width // block
    depth6 = ortho6.shape[1]
    parts = 8
    rows = tokens // parts

    def body(got_ref, acts_ref, error_ref, ortho_ref, basis_ref, out_ref, columns, held, sems):
        n = pl.program_id(0)
        slot = lax.rem(n, 2)

        def copies(m, s):
            place = pl.ds(pl.multiple_of(m * block, block), block)
            pieces = [pl.ds(k * rows, rows) for k in range(parts)]
            return [pltpu.make_async_copy(acts_ref.at[p, place], held.at[s, p], sems.at[s, k]) for k, p in enumerate(pieces)]

        def close(total):
            out_ref[...] = (total * scale + error_ref[...].astype(jnp.float32)).astype(jnp.bfloat16)

        @pl.when(n == 0)
        def _():
            for c in copies(0, 0):
                c.start()
            if steps > 1:
                for c in copies(1, 1):
                    c.start()
            columns[:, tokens:] = ortho_ref[...]
            for s in range(shards):
                columns[:, s * tok : (s + 1) * tok] = got_ref[s]
            total = jnp.dot(ortho_ref[...], basis_ref[...], preferred_element_type=jnp.float32)
            for k, c in enumerate(copies(0, 0)):
                c.wait()
                piece = slice(k * rows, (k + 1) * rows)
                total = total + jnp.dot(columns[:, piece], held[0, piece], preferred_element_type=jnp.float32)
            close(total)

        @pl.when(n > 0)
        def _():
            held[slot, tokens:] = basis_ref[...]
            for c in copies(n, slot):
                c.wait()
            close(jnp.dot(columns[...], held[slot], preferred_element_type=jnp.float32))

        @pl.when(n + 2 < steps)
        def _():
            for c in copies(n + 2, slot):
                c.start()

    wide = pl.BlockSpec((cols, block), lambda n: (0, n))
    return pl.pallas_call(
        body,
        out_shape=jax.ShapeDtypeStruct(error_t.shape, jnp.bfloat16),
        grid=(steps,),
        in_specs=[
            pl.BlockSpec((shards, cols, tok), lambda n: (0, 0, 0)),
            pl.BlockSpec(memory_space=pl.ANY),
            wide,
            pl.BlockSpec((cols, depth6), lambda n: (0, 0)),
            pl.BlockSpec((depth6, block), lambda n: (0, n)),
        ],
        out_specs=wide,
        scratch_shapes=[
            pltpu.VMEM((cols, tokens + depth6), got.dtype),
            pltpu.VMEM((2, tokens + depth6, block), gathered.dtype),
            pltpu.SemaphoreType.DMA((2, parts)),
        ],
        compiler_params=pltpu.CompilerParams(vmem_limit_bytes=VMEM_LIMIT),
        cost_estimate=pl.CostEstimate(
            flops=2 * cols * width * (tokens + depth6), bytes_accessed=2 * tokens * (width + cols) + 4 * cols * width, transcendentals=0
        ),
    )(got, gathered, error_t, ortho6, basis6)


def adam(place, ortho6, basis6, weight, moment_one, moment_two, scale):
    cols, rows = weight.shape
    block = min(512, rows)
    steps = rows // block
    depth6 = ortho6.shape[1]

    def body(p, ortho_ref, basis_ref, w_ref, one_ref, two_ref, w_out, one_out, two_out):
        update = jnp.dot(ortho_ref[...], basis_ref[...], preferred_element_type=jnp.float32) * (-scale)
        one = beta_one * one_ref[...] + (1.0 - beta_one) * update
        two = beta_two * two_ref[...] + (1.0 - beta_two) * update * update
        root = jnp.sqrt(two * (1.0 / second_fix)) + adam_epsilon
        step = one * (learn_rate / first_fix) / root
        w_out[...] = w_ref[...] * (1.0 - learn_rate * decay_rate) - step
        one_out[...] = one
        two_out[...] = two

    own = pl.BlockSpec((cols, block), lambda n, p: (0, n))
    return pl.pallas_call(
        body,
        out_shape=[jax.ShapeDtypeStruct(weight.shape, jnp.float32)] * 3,
        grid_spec=pltpu.PrefetchScalarGridSpec(
            num_scalar_prefetch=1,
            grid=(steps,),
            in_specs=[
                pl.BlockSpec((cols, depth6), lambda n, p: (0, 0)),
                pl.BlockSpec((depth6, block), lambda n, p: (0, p[0] * steps + n)),
                own,
                own,
                own,
            ],
            out_specs=[own, own, own],
        ),
        compiler_params=pltpu.CompilerParams(vmem_limit_bytes=20 * 1024 * 1024),
        cost_estimate=pl.CostEstimate(flops=2 * cols * rows * depth6, bytes_accessed=24 * cols * rows, transcendentals=cols * rows),
    )(place, ortho6, basis6, weight, moment_one, moment_two)


def per_device(acts, grads, basis, error_in, weight, moment_one, moment_two):
    highest = lax.Precision.HIGHEST
    shards = lax.axis_size(SHARD)
    chips = lax.axis_size(CHIPS)
    pods = lax.axis_size("outer")
    tok, width = acts.shape
    cols = error_in.shape[2]
    rank = basis.shape[0]
    scale = (tok * shards) ** (-0.5)
    core = lax.axis_index("core")
    error_t = error_in[0].T
    gathered = lax.all_gather(acts, SHARD, axis=0, tiled=True)

    proj = gather_axis(thrice(basis, acts, 1) * scale, "y")
    grads_t, proj = lax.optimization_barrier((grads.T.reshape(shards, cols, tok), proj))
    got = lax.all_to_all(grads_t, SHARD, 0, 0)
    got_t = got.transpose(1, 0, 2).reshape(cols, shards * tok)
    base = thrice(basis, error_t, 1)
    proj, base = lax.optimization_barrier((gather_axis(proj, "z"), base))
    other = twin(proj)
    proj = jnp.stack([jnp.where(core == 0, proj, other), jnp.where(core == 0, other, proj)], 2)
    proj = proj.transpose(3, 0, 1, 2, 4).reshape(rank, shards * tok)

    factor = sum4(thrice(proj, got_t, 1) + base, "outer") / pods
    factor3 = jnp.concatenate(split3(factor), 0)
    keep, send = project(core.astype(jnp.int32).reshape(1), factor, factor3, got)
    inner = lax.all_to_all(keep + twin(send), ("z", "y"), 0, 0, tiled=True).sum(0)
    gram = jnp.concatenate([inner[rank:, i : i + rank] for i in range(0, tok, rank)], 0)
    terms = thrice(inner[:rank] * scale, acts, 0) + thrice(factor, error_t, 0)

    half = width // 2
    mine = lax.dynamic_slice_in_dim(terms, core * half, half, 1)
    other = lax.dynamic_slice_in_dim(terms, (1 - core) * half, half, 1)
    mine = scatter4((mine + twin(other)).reshape(pods, rank // pods, half), "outer")
    mine, gram = lax.optimization_barrier((mine, gram))
    mine = mine.reshape(rank // pods, chips // pods, -1).transpose(1, 0, 2)
    piece = lax.all_to_all(mine, ("z", "y"), 0, 0, tiled=True).sum(0) / pods
    mine = lax.all_to_all(jnp.broadcast_to(piece[None], (chips,) + piece.shape), CHIPS, 0, 0, tiled=True)
    mine = mine.reshape((pods, chips // pods) + piece.shape)
    other = twin(mine)
    terms = jnp.concatenate([jnp.where(core == 0, mine, other), jnp.where(core == 0, other, mine)], 1)
    terms = terms.transpose(0, 2, 1, 3).reshape(rank, width)

    lower = jnp.linalg.cholesky(gram)
    inverse = jax.scipy.linalg.solve_triangular(lower, jnp.eye(rank, dtype=jnp.float32), lower=True)
    ortho = jnp.dot(inverse, factor, precision=highest)
    basis_out = jnp.dot(inverse, terms, precision=highest)

    oh, om, ol = split3(ortho)
    bh, bm, bl = split3(basis_out * (-1.0 / scale))
    zero = jnp.zeros_like(bh)
    ortho6 = jnp.concatenate([oh, oh, om, oh, ol, om, jnp.zeros_like(oh), jnp.zeros_like(oh)], 0).T
    basis6 = jnp.concatenate([bh, bm, bh, bl, bh, bm, zero, zero], 0)

    place = lax.axis_index("outer").astype(jnp.int32).reshape(1)
    state = adam(place, ortho6, basis6, weight.T, moment_one.T, moment_two.T, scale)
    error_out = finish_error(got, gathered, error_t, ortho6, basis6, scale)
    return (basis_out, error_out.T[None], state[0].T, state[1].T, state[2].T)


def solution(mesh):
    devices = mesh.devices
    mesh = Mesh(devices.reshape(devices.shape[0], 4, 4, -1), ALL)
    tokens = P(ALL, None)
    state = P("outer", SHARD)
    errors = P("outer", None, SHARD)
    return jax.shard_map(
        per_device,
        mesh=mesh,
        in_specs=(tokens, tokens, P(), errors, state, state, state),
        out_specs=(P(), errors, state, state, state),
        check_vma=False,
    )
```

```python
import jax
import jax.numpy as jnp
from jax import lax
from jax.experimental import pallas as pl
from jax.experimental.pallas import tpu as pltpu
from jax.sharding import Mesh, PartitionSpec as P

beta_one = 0.9
beta_two = 0.95
learn_rate = 0.01
decay_rate = 0.1
adam_epsilon = 1e-08
first_fix = 1.0 - 0.9**8
second_fix = 1.0 - 0.95**8

SHARD = ("z", "y", "core")
ALL = ("outer", "z", "y", "core")
CHIPS = ("outer", "z", "y")
VMEM_LIMIT = 48 * 1024 * 1024


def split3(x):
    high = lax.reduce_precision(x, 8, 7)
    rest = x - high
    middle = lax.reduce_precision(rest, 8, 7)
    return [p.astype(jnp.bfloat16) for p in (high, middle, rest - middle)]


def dot(a, b, ca, cb):
    return lax.dot_general(a, b, (((ca,), (cb,)), ((), ())), preferred_element_type=jnp.float32)


def thrice(x, b, cb):
    r = x.shape[0]
    y = dot(jnp.concatenate(split3(x), 0), b, 1, cb)
    return y[:r] + y[r : 2 * r] + y[2 * r :]


def swap(x, axis, k):
    return lax.ppermute(x, axis, [(i, i ^ k) for i in range(lax.axis_size(axis))])


def twin(x):
    return swap(x, "core", 1)


def sum4(x, axis):
    a, b, c = swap(x, axis, 1), swap(x, axis, 2), swap(x, axis, 3)
    return (x + a) + (b + c)


def scatter4(x, axis):
    i = lax.axis_index(axis)
    own, a, b, c = (lax.dynamic_index_in_dim(x, i ^ k, 0, keepdims=False) for k in range(4))
    a, b, c = (swap(v, axis, k) for v, k in ((a, 1), (b, 2), (c, 3)))
    return (own + a) + (b + c)


def gather_axis(x, axis):
    n = lax.axis_size(axis)
    i = lax.axis_index(axis)
    x = jnp.stack([x] + [swap(x, axis, k) for k in range(1, n)])
    bit = 1
    while bit < n:
        y = x.reshape((n // (2 * bit), 2, bit) + x.shape[1:])
        x = jnp.where((i & bit) != 0, y[:, ::-1], y).reshape(x.shape)
        bit *= 2
    return x


def parts3(x):
    high = x.astype(jnp.bfloat16)
    rest = x - high.astype(jnp.float32)
    middle = rest.astype(jnp.bfloat16)
    return high, middle, (rest - middle.astype(jnp.float32)).astype(jnp.bfloat16)


def project(core, factor, factor3, got):
    shards, cols, tok = got.shape
    rank = factor.shape[0]
    chips = shards // 2
    step = min(8, chips)
    extra = rank * rank // tok

    def body(c, f_ref, f3_ref, g_ref, keep_ref, send_ref, gram_ref):
        own = c[0] == 0

        @pl.when(pl.program_id(0) == 0)
        def _():
            h, m, l = parts3(f_ref[...])
            gram = dot(h, l, 1, 1) + dot(l, h, 1, 1) + dot(m, m, 1, 1)
            gram = gram + (dot(h, m, 1, 1) + dot(m, h, 1, 1)) + dot(h, h, 1, 1)
            gram_ref[...] = jnp.concatenate([gram[i * extra : (i + 1) * extra] for i in range(rank // extra)], axis=1)

        for k in range(step):
            pair = jnp.concatenate([g_ref[2 * k], g_ref[2 * k + 1]], axis=1)
            y = jnp.dot(f3_ref[...], pair, preferred_element_type=jnp.float32)
            y = y[:rank] + y[rank : 2 * rank] + y[2 * rank :]
            first, second = y[:, :tok], y[:, tok:]
            keep_ref[k, :rank] = jnp.where(own, first, second)
            send_ref[k, :rank] = jnp.where(own, second, first)
            keep_ref[k, rank:] = gram_ref[...]
            send_ref[k, rank:] = gram_ref[...]

    block = pl.BlockSpec((step, rank + extra, tok), lambda n, c: (n, 0, 0))
    return pl.pallas_call(
        body,
        out_shape=[jax.ShapeDtypeStruct((chips, rank + extra, tok), jnp.float32)] * 2,
        grid_spec=pltpu.PrefetchScalarGridSpec(
            num_scalar_prefetch=1,
            grid=(chips // step,),
            in_specs=[
                pl.BlockSpec((rank, cols), lambda n, c: (0, 0)),
                pl.BlockSpec((3 * rank, cols), lambda n, c: (0, 0)),
                pl.BlockSpec((2 * step, cols, tok), lambda n, c: (n, 0, 0)),
            ],
            out_specs=[block, block],
            scratch_shapes=[pltpu.VMEM((extra, tok), jnp.float32)],
        ),
        compiler_params=pltpu.CompilerParams(vmem_limit_bytes=VMEM_LIMIT),
        cost_estimate=pl.CostEstimate(flops=6 * rank * cols * shards * tok, bytes_accessed=2 * shards * cols * tok, transcendentals=0),
    )(core, factor, factor3, got)


def finish_error(got, gathered, error_t, ortho6, basis6, scale):
    shards, cols, tok = got.shape
    tokens, width = gathered.shape
    block = min(1024, width)
    steps = width // block
    depth6 = ortho6.shape[1]
    parts = 8
    rows = tokens // parts

    def body(got_ref, acts_ref, error_ref, ortho_ref, basis_ref, out_ref, columns, held, sems):
        n = pl.program_id(0)
        slot = lax.rem(n, 2)

        def copy(m, s, k):
            piece = pl.ds(k * rows, rows)
            place = pl.ds(pl.multiple_of(m * block, block), block)
            return pltpu.make_async_copy(acts_ref.at[piece, place], held.at[s, piece], sems.at[s, k])

        def close(gradient):
            approx = jnp.dot(ortho_ref[...], basis_ref[...], preferred_element_type=jnp.float32)
            matrix = gradient * scale + error_ref[...].astype(jnp.float32)
            out_ref[...] = (matrix - approx).astype(jnp.bfloat16)

        @pl.when(n == 0)
        def _():
            for k in range(parts):
                copy(0, 0, k).start()
            if steps > 1:
                for k in range(parts):
                    copy(1, 1, k).start()
            for s in range(shards):
                columns[:, s * tok : (s + 1) * tok] = got_ref[s]
            total = None
            for k in range(parts):
                copy(0, 0, k).wait()
                piece = slice(k * rows, (k + 1) * rows)
                d = jnp.dot(columns[:, piece], held[0, piece], preferred_element_type=jnp.float32)
                total = d if total is None else total + d
            close(total)

        @pl.when(n > 0)
        def _():
            for k in range(parts):
                copy(n, slot, k).wait()
            close(jnp.dot(columns[...], held[slot], preferred_element_type=jnp.float32))

        @pl.when(n + 2 < steps)
        def _():
            for k in range(parts):
                copy(n + 2, slot, k).start()

    wide = pl.BlockSpec((cols, block), lambda n: (0, n))
    return pl.pallas_call(
        body,
        out_shape=jax.ShapeDtypeStruct(error_t.shape, jnp.bfloat16),
        grid=(steps,),
        in_specs=[
            pl.BlockSpec((shards, cols, tok), lambda n: (0, 0, 0)),
            pl.BlockSpec(memory_space=pl.ANY),
            wide,
            pl.BlockSpec((cols, depth6), lambda n: (0, 0)),
            pl.BlockSpec((depth6, block), lambda n: (0, n)),
        ],
        out_specs=wide,
        scratch_shapes=[
            pltpu.VMEM((cols, tokens), got.dtype),
            pltpu.VMEM((2, tokens, block), gathered.dtype),
            pltpu.SemaphoreType.DMA((2, parts)),
        ],
        compiler_params=pltpu.CompilerParams(vmem_limit_bytes=VMEM_LIMIT),
        cost_estimate=pl.CostEstimate(
            flops=2 * cols * width * (tokens + depth6), bytes_accessed=2 * tokens * (width + cols) + 4 * cols * width, transcendentals=0
        ),
    )(got, gathered, error_t, ortho6, basis6)


def adam(place, ortho6, basis6, weight, moment_one, moment_two):
    cols, rows = weight.shape
    block = min(512, rows)
    steps = rows // block
    depth6 = ortho6.shape[1]

    def body(p, ortho_ref, basis_ref, w_ref, one_ref, two_ref, w_out, one_out, two_out):
        update = jnp.dot(ortho_ref[...], basis_ref[...], preferred_element_type=jnp.float32)
        one = beta_one * one_ref[...] + (1.0 - beta_one) * update
        two = beta_two * two_ref[...] + (1.0 - beta_two) * update * update
        root = jnp.sqrt(two * (1.0 / second_fix)) + adam_epsilon
        step = one * (learn_rate / first_fix) / root
        w_out[...] = w_ref[...] * (1.0 - learn_rate * decay_rate) - step
        one_out[...] = one
        two_out[...] = two

    own = pl.BlockSpec((cols, block), lambda n, p: (0, n))
    return pl.pallas_call(
        body,
        out_shape=[jax.ShapeDtypeStruct(weight.shape, jnp.float32)] * 3,
        grid_spec=pltpu.PrefetchScalarGridSpec(
            num_scalar_prefetch=1,
            grid=(steps,),
            in_specs=[
                pl.BlockSpec((cols, depth6), lambda n, p: (0, 0)),
                pl.BlockSpec((depth6, block), lambda n, p: (0, p[0] * steps + n)),
                own,
                own,
                own,
            ],
            out_specs=[own, own, own],
        ),
        compiler_params=pltpu.CompilerParams(vmem_limit_bytes=20 * 1024 * 1024),
        cost_estimate=pl.CostEstimate(flops=2 * cols * rows * depth6, bytes_accessed=24 * cols * rows, transcendentals=cols * rows),
    )(place, ortho6, basis6, weight, moment_one, moment_two)


def per_device(acts, grads, basis, error_in, weight, moment_one, moment_two):
    highest = lax.Precision.HIGHEST
    shards = lax.axis_size(SHARD)
    chips = lax.axis_size(CHIPS)
    pods = lax.axis_size("outer")
    tok, width = acts.shape
    cols = error_in.shape[2]
    rank = basis.shape[0]
    scale = (tok * shards) ** (-0.5)
    core = lax.axis_index("core")
    error_t = error_in[0].T
    gathered = lax.all_gather(acts, SHARD, axis=0, tiled=True)

    proj = gather_axis(thrice(basis, acts, 1) * scale, "y")
    grads_t, proj = lax.optimization_barrier((grads.T.reshape(shards, cols, tok), proj))
    got = lax.all_to_all(grads_t, SHARD, 0, 0)
    got_t = got.transpose(1, 0, 2).reshape(cols, shards * tok)
    base = thrice(basis, error_t, 1)
    proj, base = lax.optimization_barrier((gather_axis(proj, "z"), base))
    other = twin(proj)
    proj = jnp.stack([jnp.where(core == 0, proj, other), jnp.where(core == 0, other, proj)], 2)
    proj = proj.transpose(3, 0, 1, 2, 4).reshape(rank, shards * tok)

    factor = sum4(thrice(proj, got_t, 1) + base, "outer") / pods
    factor3 = jnp.concatenate(split3(factor), 0)
    keep, send = project(core.astype(jnp.int32).reshape(1), factor, factor3, got)
    inner = lax.all_to_all(keep + twin(send), ("z", "y"), 0, 0, tiled=True).sum(0)
    gram = jnp.concatenate([inner[rank:, i : i + rank] for i in range(0, tok, rank)], 0)
    terms = thrice(inner[:rank] * scale, acts, 0) + thrice(factor, error_t, 0)

    half = width // 2
    mine = lax.dynamic_slice_in_dim(terms, core * half, half, 1)
    other = lax.dynamic_slice_in_dim(terms, (1 - core) * half, half, 1)
    mine = scatter4((mine + twin(other)).reshape(pods, rank // pods, half), "outer")
    mine, gram = lax.optimization_barrier((mine, gram))
    mine = mine.reshape(rank // pods, chips // pods, -1).transpose(1, 0, 2)
    piece = lax.all_to_all(mine, ("z", "y"), 0, 0, tiled=True).sum(0) / pods
    mine = lax.all_to_all(jnp.broadcast_to(piece[None], (chips,) + piece.shape), CHIPS, 0, 0, tiled=True)
    mine = mine.reshape((pods, chips // pods) + piece.shape)
    other = twin(mine)
    terms = jnp.concatenate([jnp.where(core == 0, mine, other), jnp.where(core == 0, other, mine)], 1)
    terms = terms.transpose(0, 2, 1, 3).reshape(rank, width)

    lower = jnp.linalg.cholesky(gram)
    inverse = jax.scipy.linalg.solve_triangular(lower, jnp.eye(rank, dtype=jnp.float32), lower=True)
    ortho = jnp.dot(inverse, factor, precision=highest)
    basis_out = jnp.dot(inverse, terms, precision=highest)

    oh, om, ol = split3(ortho)
    bh, bm, bl = split3(basis_out)
    ortho6 = jnp.concatenate([oh, oh, om, oh, ol, om], 0).T
    basis6 = jnp.concatenate([bh, bm, bh, bl, bh, bm], 0)

    place = lax.axis_index("outer").astype(jnp.int32).reshape(1)
    state = adam(place, ortho6, basis6, weight.T, moment_one.T, moment_two.T)
    error_out = finish_error(got, gathered, error_t, ortho6, basis6, scale)
    return (basis_out, error_out.T[None], state[0].T, state[1].T, state[2].T)


def solution(mesh):
    devices = mesh.devices
    mesh = Mesh(devices.reshape(devices.shape[0], 4, 4, -1), ALL)
    tokens = P(ALL, None)
    state = P("outer", SHARD)
    errors = P("outer", None, SHARD)
    return jax.shard_map(
        per_device,
        mesh=mesh,
        in_specs=(tokens, tokens, P(), errors, state, state, state),
        out_specs=(P(), errors, state, state, state),
        check_vma=False,
    )
```
